32 devices in a mesh: lat: 16 (over z, y, core), chan: 2 (over x).
Axes of the slice: x: 2, y: 2, z: 4, core: 2. Of those that a mesh axis runs over, the one named last changes fastest.
Arguments:
- fields: float32 [32, 900, 768], P(('lat', 'chan')), may hold values from -6 to 6
- first_gain: float32 [768], replicated, may hold values from 0.5 to 1.5
- first_shift: float32 [768], replicated, may hold values from -1.5 to 1.5
- filter_one: float32 [8, 2, 96, 96], P('chan'), may hold values from -0.4375 to 0.4375
- filter_one_bias: float32 [8, 2, 96], P('chan'), may hold values from -2.5 to 2.5
- filter_two: float32 [8, 2, 96, 96], P('chan'), may hold values from -0.4375 to 0.4375
- filter_two_bias: float32 [8, 2, 96], P('chan'), may hold values from -2.5 to 2.5
- second_gain: float32 [768], replicated, may hold values from 0.5 to 1.5
- second_shift: float32 [768], replicated, may hold values from -1.5 to 1.5
- dense_weights: bfloat16 [3072, 2, 768], P(('lat', 'chan')), may hold values from -0.21875 to 0.21875
- dense_bias: bfloat16 [3072], P(('lat', 'chan')), may hold values from -2.5 to 2.5
- output_bias: float32 [768], replicated, may hold values from -1.5 to 1.5
Outputs:
- block_output: float32 [32, 900, 768], P(('lat', 'chan'))
The draws below stay inside these ranges and needn't reach their ends.
All inputs are finite; a program needn't handle non-finite values.
Results may differ from the reference program's by a relative error of at most 0.0025.
Values may be sent and summed in bfloat16 or wider, within the bound.
A program may use at most 128 MiB of HBM per device.

```python
import jax
import jax.numpy as jnp
from jax import lax

C = 768
NB = 8
BS = 96
FF = 3072
W = 900
KW = 256
H = 32


def block_levels(own_key, extent, split, least, largest):
    level = 1.0
    for position, blocks in split:
        steps = jax.random.uniform(jax.random.fold_in(jax.random.fold_in(own_key, 6), position), (blocks,), jnp.float32, least / len(split), largest / len(split))
        level = level * jnp.repeat(jnp.exp(steps), extent[position] // blocks).reshape((-1,) + (1,) * (len(extent) - 1 - position))
    return level


def normal_values(own_key, shape, spread, reach, split=(), dtype=jnp.bfloat16):
    gain = block_levels(own_key, shape, split, -0.22, 0.18) if split else 1.0
    drawn = jax.random.normal(own_key, shape, jnp.float32) * spread * gain
    return jnp.minimum(jnp.maximum(drawn, -reach), reach).astype(dtype)


def setup_inputs(seed: int = 0) -> dict:
    seeds = jax.random.split(jax.random.key(seed), 13)
    fields = normal_values(seeds[0], (H, W, C), 1.0, 6.0, ((0, 32),), jnp.float32)
    first_gain = jnp.clip(1.0 + 0.1 * jax.random.normal(seeds[1], (C,), jnp.float32), 0.5, 1.5)
    first_shift = normal_values(seeds[2], (C,), 0.3, 1.5, (), jnp.float32)
    filter_one = normal_values(seeds[3], (NB, 2, BS, BS), (2 * BS) ** -0.5, 0.4375, ((0, 2),), jnp.float32)
    filter_one_bias = normal_values(seeds[4], (NB, 2, BS), 0.5, 2.5, ((0, 2),), jnp.float32)
    filter_two = normal_values(seeds[5], (NB, 2, BS, BS), (2 * BS) ** -0.5, 0.4375, ((0, 2),), jnp.float32)
    filter_two_bias = normal_values(seeds[6], (NB, 2, BS), 0.5, 2.5, ((0, 2),), jnp.float32)
    second_gain = jnp.clip(1.0 + 0.1 * jax.random.normal(seeds[7], (C,), jnp.float32), 0.5, 1.5)
    second_shift = normal_values(seeds[8], (C,), 0.3, 1.5, (), jnp.float32)
    dense_weights = normal_values(seeds[9], (FF, 2, C), C ** -0.5, 0.21875, ((0, 32),))
    dense_bias = normal_values(seeds[10], (FF,), 0.5, 2.5, ((0, 32),))
    output_bias = normal_values(seeds[11], (C,), 0.3, 1.5, (), jnp.float32)
    return {"fields": fields, "first_gain": first_gain, "first_shift": first_shift, "filter_one": filter_one, "filter_one_bias": filter_one_bias, "filter_two": filter_two, "filter_two_bias": filter_two_bias, "second_gain": second_gain, "second_shift": second_shift, "dense_weights": dense_weights, "dense_bias": dense_bias, "output_bias": output_bias}


exact_mode = lax.Precision.HIGHEST
norm_eps = 1e-05
shrink_level = 0.01

def layer_norm(values, gain_terms, shift_terms):
    mean_value = lax.optimization_barrier(jnp.mean(values, axis=-1, keepdims=True))
    centered = values - mean_value
    variance = lax.optimization_barrier(jnp.mean(centered * centered, axis=-1, keepdims=True))
    return centered * lax.rsqrt(variance + norm_eps) * gain_terms + shift_terms

def complex_layer(real_part, imag_part, weight, bias_terms):
    real_weight = weight[:, 0]
    imag_weight = weight[:, 1]
    out_real = jnp.einsum('hkni,nio->hkno', real_part, real_weight, precision=exact_mode) - jnp.einsum('hkni,nio->hkno', imag_part, imag_weight, precision=exact_mode) + bias_terms[:, 0]
    out_imag = jnp.einsum('hkni,nio->hkno', imag_part, real_weight, precision=exact_mode) + jnp.einsum('hkni,nio->hkno', real_part, imag_weight, precision=exact_mode) + bias_terms[:, 1]
    return (out_real, out_imag)

def soft_shrink(values):
    return jnp.sign(values) * jnp.maximum(jnp.abs(values) - shrink_level, 0.0)

def reference(fields, first_gain, first_shift, filter_one, filter_one_bias, filter_two, filter_two_bias, second_gain, second_shift, dense_weights, dense_bias, output_bias):
    normed_in = layer_norm(fields, first_gain, first_shift)
    lon_modes = jnp.fft.rfft(normed_in, axis=1, norm='ortho')[:, :KW, :]
    spectrum = jnp.fft.fft(lon_modes, axis=0, norm='ortho')
    real_part = jnp.real(spectrum).reshape(H, KW, NB, BS)
    imag_part = jnp.imag(spectrum).reshape(H, KW, NB, BS)
    real_part, imag_part = complex_layer(real_part, imag_part, filter_one, filter_one_bias)
    real_part = jnp.maximum(real_part, 0.0)
    imag_part = jnp.maximum(imag_part, 0.0)
    real_part, imag_part = complex_layer(real_part, imag_part, filter_two, filter_two_bias)
    real_part = soft_shrink(real_part)
    imag_part = soft_shrink(imag_part)
    mixed_modes = (real_part + 1j * imag_part).reshape(H, KW, C)
    lat_back = jnp.fft.ifft(mixed_modes, axis=0, norm='ortho')
    padded = jnp.pad(lat_back, ((0, 0), (0, W // 2 + 1 - KW), (0, 0)))
    filtered = jnp.fft.irfft(padded, n=W, axis=1, norm='ortho') + normed_in
    summed = filtered + fields

    def dense_row(row_values):
        row_normed = layer_norm(row_values, second_gain, second_shift).astype(jnp.bfloat16)
        pre_act = lax.dot_general(row_normed, dense_weights[:, 0, :], (((1,), (1,)), ((), ())), preferred_element_type=jnp.float32) + dense_bias.astype(jnp.float32)
        hidden = jax.nn.gelu(pre_act, approximate=False).astype(jnp.bfloat16)
        dense_out = jnp.dot(hidden, dense_weights[:, 1, :], preferred_element_type=jnp.float32)
        return row_values + (dense_out + output_bias)
    return lax.map(dense_row, summed)
```

```python
import jax
import jax.numpy as jnp
import numpy as np
from jax import lax
from jax.sharding import PartitionSpec as P

KW = 256


split_mode = lax.Precision.HIGH
norm_eps = 1e-05
shrink_level = 0.01


def layer_norm(values, gain_terms, shift_terms):
    mean_value = jnp.mean(values, axis=-1, keepdims=True)
    centered = values - mean_value
    variance = jnp.mean(centered * centered, axis=-1, keepdims=True)
    return centered * lax.rsqrt(variance + norm_eps) * gain_terms + shift_terms


def soft_shrink(values):
    return jnp.sign(values) * jnp.maximum(jnp.abs(values) - shrink_level, 0.0)


def block_matrix(weight):
    blocks, _, size, _ = weight.shape
    same_block = jnp.eye(blocks, dtype=weight.dtype)
    spread = jnp.einsum("npio,nq->pniqo", weight, same_block, precision=lax.Precision.HIGHEST)
    spread = spread.reshape(2, blocks * size, blocks * size)
    upper = jnp.concatenate([spread[0], spread[1]], axis=1)
    lower = jnp.concatenate([-spread[1], spread[0]], axis=1)
    return jnp.concatenate([upper, lower], axis=0)


def turn(first, second, period):
    angle = 2.0 * np.pi / period * ((first[:, None] * second[None, :]) % period)
    return np.cos(angle), np.sin(angle)


def product(left, right):
    return jnp.dot(left, right, precision=split_mode, preferred_element_type=jnp.float32)


def lon_matrices(width, lat_count):
    local_modes = KW // lat_count
    cos_part, sin_part = turn(np.arange(KW), np.arange(width), width)
    pair = np.stack([cos_part, -sin_part]).reshape(2, lat_count, local_modes, width)
    pair = pair.transpose(1, 0, 2, 3) * width**-0.5
    factor = np.where(np.arange(KW) == 0, 1.0, 2.0).reshape(lat_count, 1, local_modes, 1)
    forward = pair.reshape(2 * KW, width)
    inverse = (pair * factor).reshape(2 * KW, width)
    return forward.astype(np.float32), np.ascontiguousarray(inverse.T).astype(np.float32)


def lat_matrices(height):
    cos_part, sin_part = turn(np.arange(height), np.arange(height), height)
    forward = np.stack([np.stack([cos_part, sin_part], 1), np.stack([-sin_part, cos_part], 1)])
    inverse = np.stack([np.stack([cos_part, -sin_part], 1), np.stack([sin_part, cos_part], 1)])
    return forward * height**-0.5, inverse * height**-0.5


def per_device(
    fields,
    first_gain,
    first_shift,
    filter_one,
    filter_one_bias,
    filter_two,
    filter_two_bias,
    second_gain,
    second_shift,
    dense_weights,
    dense_bias,
    output_bias,
):
    row_count, width, channels = fields.shape
    lat_count = lax.axis_size("lat")
    chan_count = lax.axis_size("chan")
    devices = lat_count * chan_count
    height = row_count * devices
    local_modes = KW // lat_count
    local_channels = channels // chan_count
    hidden_share = dense_weights.shape[0]
    both = ("lat", "chan")

    packed = jnp.concatenate(
        [
            dense_weights.reshape(hidden_share, 2 * channels),
            jnp.broadcast_to(dense_bias[:, None], (hidden_share, 128)),
        ],
        axis=1,
    )
    gathered = lax.all_gather(packed, both, axis=0, tiled=True)

    forward_lon, inverse_lon = lon_matrices(width, lat_count)
    forward_lat, inverse_lat = lat_matrices(height)
    normed_in = layer_norm(fields, first_gain, first_shift)
    lon_modes = jnp.stack([product(forward_lon, normed_in[r]) for r in range(row_count)])
    lon_modes = lon_modes.astype(jnp.bfloat16).reshape(
        row_count, lat_count, 2 * local_modes, chan_count, local_channels
    )
    sent = lon_modes.transpose(1, 3, 0, 2, 4).reshape(
        devices, row_count * 2 * local_modes, local_channels
    )
    moved = lax.all_to_all(sent, both, split_axis=0, concat_axis=0, tiled=True)
    moved = moved.astype(jnp.float32)
    rows = height * local_modes
    if rows <= 1024:
        mode_eye = np.eye(local_modes)
        spread_forward = np.einsum("bmah,kl->bmkhal", forward_lat, mode_eye).reshape(2, rows, 2 * rows)
        spread_inverse = np.einsum("ahbm,kl->hakbml", inverse_lat, mode_eye).reshape(2 * rows, 2, rows)
        flat = moved.reshape(2 * rows, local_channels)
        real_part = product(spread_forward[0].astype(np.float32), flat)
        imag_part = product(spread_forward[1].astype(np.float32), flat)
    else:
        parted = moved.reshape(height, 2, local_modes, local_channels)
        parts = jnp.einsum(
            "bmah,hakc->bmkc", forward_lat.astype(np.float32), parted, precision=split_mode
        ).reshape(2, rows, local_channels)
        real_part, imag_part = parts[0], parts[1]
    spectrum = jnp.concatenate([real_part, imag_part], axis=1)
    one_bias = filter_one_bias.transpose(1, 0, 2).reshape(-1)
    two_bias = filter_two_bias.transpose(1, 0, 2).reshape(-1)
    first_out = jnp.maximum(product(spectrum, block_matrix(filter_one)) + one_bias, 0.0)
    second_out = soft_shrink(product(first_out, block_matrix(filter_two)) + two_bias)
    real_out = second_out[:, :local_channels]
    imag_out = second_out[:, local_channels:]
    if rows <= 1024:
        lat_back = product(spread_inverse[:, 0].astype(np.float32), real_out) + product(
            spread_inverse[:, 1].astype(np.float32), imag_out
        )
    else:
        parted = jnp.stack([real_out, imag_out]).reshape(2, height, local_modes, local_channels)
        lat_back = jnp.einsum(
            "ahbm,bmkc->hakc", inverse_lat.astype(np.float32), parted, precision=split_mode
        )
    lat_back = lat_back.astype(jnp.bfloat16).reshape(
        devices, row_count * 2 * local_modes, local_channels
    )
    returned = lax.all_to_all(lat_back, both, split_axis=0, concat_axis=0, tiled=True)
    returned = returned.reshape(lat_count, chan_count, row_count, 2 * local_modes, local_channels)
    returned = returned.transpose(2, 0, 3, 1, 4).reshape(row_count, 2 * KW, channels)
    returned = returned.astype(jnp.float32)
    back = jnp.stack([product(inverse_lon, returned[r]) for r in range(row_count)])
    summed = back + normed_in + fields
    flat_normed = layer_norm(summed, second_gain, second_shift).astype(jnp.bfloat16)
    flat_normed = flat_normed.reshape(row_count * width, channels)
    pre_act = lax.dot_general(
        flat_normed,
        gathered[:, :channels],
        (((1,), (1,)), ((), ())),
        preferred_element_type=jnp.float32,
    ) + gathered[:, 2 * channels].astype(jnp.float32)
    hidden = jax.nn.gelu(pre_act, approximate=False).astype(jnp.bfloat16)
    dense_out = jnp.dot(
        hidden, gathered[:, channels : 2 * channels], preferred_element_type=jnp.float32
    )
    return summed + (dense_out + output_bias).reshape(row_count, width, channels)


def solution(mesh):
    placed = (
        P(("lat", "chan"), None, None),
        P(),
        P(),
        P("chan", None, None, None),
        P("chan", None, None),
        P("chan", None, None, None),
        P("chan", None, None),
        P(),
        P(),
        P(("lat", "chan"), None, None),
        P(("lat", "chan")),
        P(),
    )
    return jax.shard_map(
        per_device,
        mesh=mesh,
        in_specs=placed,
        out_specs=P(("lat", "chan"), None, None),
        check_vma=False,
    )
```
